128 devices in a mesh: expo: 4 (over y), fp: 32 (over x, z, core).
Axes of the slice: x: 4, y: 4, z: 4, core: 2. Of those that a mesh axis runs over, the one named last changes fastest.
Arguments:
- raw_pixels: bfloat16 [4, 8192, 2048], P('expo', 'fp'), may hold values from -6 to 6
- kernel_bank: bfloat16 [8, 2, 41], replicated, may hold values from -1 to 1
- kernel_ids: int32 [4, 32], P('expo', 'fp'), may hold values from 0 to 7
- inv_var: float32 [4, 32], P('expo', 'fp'), may hold values from 0.3 to 3
- gap_start: int32 [4, 32], P('expo', 'fp'), may hold values from 0 to 224
- warp_tile: int32 [4, 8192, 16, 1], P('expo', 'fp'), may hold values from 0 to 127; in each aligned block of 4096 rows (0 to 4095, 4096 to 8191, ..., all dimensions but the last counted through in order) at most 64 rows name the same one
- warp_offset: int32 [4, 8192, 16], P('expo', 'fp'), may hold values from 0 to 4095
Outputs:
- coadd_image: float32 [128, 4096, 128], P(('expo', 'fp'))
- coadd_weight: float32 [128, 4096], P(('expo', 'fp'))
The draws below stay inside these ranges and needn't reach their ends.
Inputs may be any that keep to these rules, and one draw needn't show every extreme that they name: `warp_tile`: among the 4096 row segments of one exposure's CCD window (256 pixel rows of 16 segments each), at most 64 go to one tile, and in some windows exactly 64 do.
All inputs are finite; a program needn't handle non-finite values.
Results may differ from the reference program's by a relative error of at most 0.006.
Values may be sent and summed in bfloat16 or wider, within the bound.
A program may use at most 64 MiB of HBM per device.

```python
import math
import jax
import jax.numpy as jnp
import numpy as np
from jax import lax

ROWS = 256
COLS = 2048
TAPS = 41
SEG = 128
KBANK = 8
GAP = 32
EXPOSURES = 4
NROWS = 8192
SEGS = 16
TILES = 128
TILE_SLOTS = 4096
CAP = 64
N_FP = 32


def touch_ends(array, own_key, least, high):
    extent = array.shape
    spot = [jax.random.randint(jax.random.fold_in(own_key, axis), (), 0, extent[axis]) for axis in range(len(extent))]
    array = array.at[tuple(spot)].set(least)
    longest = extent.index(max(extent))
    spot[longest] = (spot[longest] + 1) % extent[longest]
    return array.at[tuple(spot)].set(high)


def steps_of(stream_key, shape, cuts, low, largest):
    def one(axis_at, parts):
        draws = jax.random.uniform(jax.random.fold_in(jax.random.fold_in(stream_key, 6), axis_at), (parts,), jnp.float32, low / len(cuts), largest / len(cuts))
        return jnp.repeat(jnp.exp(draws), shape[axis_at] // parts).reshape((-1,) + (1,) * (len(shape) - axis_at - 1))

    level = one(*cuts[0])
    for cut in cuts[1:]:
        level = level * one(*cut)
    return level


def deal_out(own_key, own, number, rows, number_of, top, most, lean):
    sequence = jax.random.permutation(own_key, number_of)
    heavy_load, usual = portions_of(number_of, rows * top, most, lean, True), portions_of(number_of, rows * top, most, lean, False)
    places = jnp.arange(number_of)

    def named(lengths, turn):
        used = int((lengths > 0).sum())
        fixed = max(1, used // 4)
        passed = fixed + (places - fixed + turn * (used - fixed)) % max(1, number_of - fixed)
        return jnp.zeros((number_of,), jnp.int32).at[sequence[jnp.where(places < fixed, places, passed)]].set(jnp.asarray(lengths, jnp.int32))

    lengths = jnp.where(number % 4 == 0, named(heavy_load, number // 4), named(usual, number - number // 4 - 1))
    mixed = jax.random.permutation(jax.random.fold_in(own, 3), number_of)
    giver, sink = mixed[0:number_of // 2 * 2:2], mixed[1:number_of // 2 * 2:2]
    margin = jnp.minimum(lengths[giver] - 1, most - lengths[sink]) // 2
    margin = jnp.where((giver == sequence[0]) | (sink == sequence[0]) | (lengths[sink] == 0), 0, jnp.maximum(margin, 0))
    passed = jax.random.randint(jax.random.fold_in(own, 4), (number_of // 2,), 0, 1 << 20) % (margin + 1)
    lengths = lengths.at[giver].add(-passed).at[sink].add(passed)
    labels = jnp.searchsorted(jnp.cumsum(lengths), jnp.arange(rows * top), side="right").astype(jnp.int32)
    grid = labels.reshape(top, rows).T
    grid = grid[jax.random.permutation(jax.random.fold_in(own, 1), rows)]
    turn = jax.random.randint(jax.random.fold_in(own, 2), (rows, 1), 0, top)
    return jnp.take_along_axis(grid, (jnp.arange(top)[None, :] + turn) % top, axis=1)


def portions_of(amount, total, reach, lean, full):
    loads = [(1 << 20) // math.isqrt(standing ** lean) + 1 for standing in range(1, amount + 1)]
    largest = reach if full else min(reach, max(-(-total // amount), total * loads[0] // sum(loads)))
    least = 1 if total - largest >= amount - 1 else 0
    given, rest = [largest] + [least] * (amount - 1), total - largest - least * (amount - 1)
    while rest > 0:
        candidates = [i for i in range(1, amount) if given[i] < largest] or [i for i in range(1, amount) if given[i] < reach]
        whole, left = sum([loads[i] for i in candidates]), rest
        for i in candidates:
            addition = min(reach - given[i], max(1, left * loads[i] // whole), rest)
            given[i] = given[i] + addition
            rest = rest - addition
    return np.array(given)


def scatter_about(key, dims, scale, bound, cuts=(), held_as=jnp.bfloat16):
    drawn = scale * jax.random.normal(key, dims, jnp.float32)
    if cuts:
        drawn = drawn * steps_of(key, dims, cuts, -0.22, 0.18)
    return jnp.clip(drawn, -bound, bound).astype(held_as)


def setup_inputs(seed: int = 0) -> dict:
    splits = jax.random.split(jax.random.key(seed), 8)
    raw_pixels = scatter_about(splits[0], (EXPOSURES, NROWS, COLS), 1.0, 6.0, ((0, 4), (1, 32)))
    kernel_bank = scatter_about(splits[1], (KBANK, 2, TAPS), 0.15625, 1.0)
    kernel_ids = touch_ends(jax.random.randint(splits[2], (EXPOSURES, N_FP), 0, KBANK), jax.random.fold_in(splits[2], 1), 0, KBANK - 1).astype(jnp.int32)
    inv_var = jnp.clip(jnp.exp(math.log(3.0) - 2.3025851 * jax.random.uniform(splits[3], (EXPOSURES, N_FP), jnp.float32) ** steps_of(splits[3], (EXPOSURES, N_FP), ((0, 4), (1, 32)), -0.2, 0.2)), 0.3, 3.0)
    gap_start = touch_ends(jax.random.randint(splits[4], (EXPOSURES, N_FP), 0, ROWS - GAP + 1), jax.random.fold_in(splits[4], 1), 0, ROWS - GAP).astype(jnp.int32)
    warp_tile_keys = jax.random.split(jax.random.fold_in(splits[5], 1), EXPOSURES * NROWS * SEGS // (ROWS * SEGS))
    warp_tile_turns = jax.random.permutation(jax.random.fold_in(splits[5], 3), EXPOSURES * NROWS * SEGS // (ROWS * SEGS))
    warp_tile = jax.vmap(lambda own, number: deal_out(jax.random.fold_in(splits[5], 2), own, number, ROWS * SEGS, TILES, 1, CAP, 2))(warp_tile_keys, warp_tile_turns).reshape((EXPOSURES, NROWS, SEGS, 1))
    warp_offset = touch_ends(jax.random.randint(splits[6], (EXPOSURES, NROWS, SEGS), 0, TILE_SLOTS), jax.random.fold_in(splits[6], 1), 0, TILE_SLOTS - 1).astype(jnp.int32)
    return dict(raw_pixels=raw_pixels, kernel_bank=kernel_bank, kernel_ids=kernel_ids, inv_var=inv_var, gap_start=gap_start, warp_tile=warp_tile, warp_offset=warp_offset)


def pass_rows(frame_pixels, tap_rows):
    half_taps = tap_rows.shape[1] // 2
    padded = jnp.pad(frame_pixels.astype(jnp.float32), ((half_taps, half_taps), (0, 0)))
    running_sum = jnp.zeros(frame_pixels.shape, jnp.float32)
    for tap_index in range(tap_rows.shape[1]):
        running_sum = running_sum + tap_rows[:, tap_index:tap_index + 1].astype(jnp.float32) * padded[tap_index:tap_index + frame_pixels.shape[0]]
    return running_sum


def pass_columns(frame_pixels, tap_rows):
    half_taps = tap_rows.shape[1] // 2
    padded = jnp.pad(frame_pixels, ((0, 0), (half_taps, half_taps)))
    running_sum = jnp.zeros(frame_pixels.shape, jnp.float32)
    for tap_index in range(tap_rows.shape[1]):
        running_sum = running_sum + tap_rows[:, tap_index:tap_index + 1].astype(jnp.float32) * padded[:, tap_index:tap_index + frame_pixels.shape[1]]
    return running_sum


def reference(raw_pixels, kernel_bank, kernel_ids, inv_var, gap_start, warp_tile, warp_offset):
    slots_all = TILES * TILE_SLOTS
    row_local = jnp.arange(NROWS) % ROWS

    def exposure(running, inputs):
        frame_pixels, ids_row, weight_row, gap_row, tile_row, offset_row = inputs
        vertical_taps = jnp.repeat(kernel_bank[ids_row, 0], ROWS, axis=0)
        horizontal_taps = jnp.repeat(kernel_bank[ids_row, 1], ROWS, axis=0)
        vertical = pass_rows(frame_pixels, vertical_taps)
        vertical = lax.optimization_barrier(vertical.astype(jnp.bfloat16)).astype(jnp.float32)
        convolved = pass_columns(vertical, horizontal_taps)
        convolved = lax.optimization_barrier(convolved.astype(jnp.bfloat16)).astype(jnp.float32)
        gap_rows = jnp.repeat(gap_row, ROWS)
        in_gap = (row_local >= gap_rows) & (row_local < gap_rows + GAP)
        row_weight = jnp.where(in_gap, jnp.zeros_like(weight_row[0]), jnp.repeat(weight_row, ROWS))
        piece_weight = jnp.repeat(row_weight, SEGS)
        pieces = convolved.reshape(NROWS * SEGS, SEG)
        slot_ids = (tile_row.reshape(-1).astype(jnp.int32) * TILE_SLOTS + offset_row.reshape(-1).astype(jnp.int32)).astype(jnp.int32)
        weighted_sum, weight_sum = running
        weighted_sum = weighted_sum + jax.ops.segment_sum(piece_weight[:, None] * pieces, slot_ids, num_segments=slots_all)
        weight_sum = weight_sum + jax.ops.segment_sum(piece_weight, slot_ids, num_segments=slots_all)
        return (weighted_sum, weight_sum), None

    initial = (jnp.zeros((slots_all, SEG), jnp.float32), jnp.zeros((slots_all,), jnp.float32))
    (weighted_sum, weight_sum), ignored = lax.scan(exposure, initial, (raw_pixels, kernel_ids, inv_var, gap_start, warp_tile, warp_offset))
    coadd_image = weighted_sum / jnp.maximum(weight_sum, 1.0)[:, None]
    return coadd_image.reshape(TILES, TILE_SLOTS, SEG), weight_sum.reshape(TILES, TILE_SLOTS)
```

```python
import jax
import jax.numpy as jnp
from jax import lax
from jax.experimental import pallas as pl
from jax.experimental.pallas import tpu as pltpu
from jax.sharding import PartitionSpec as P

GAP = 32
SEG = 128
CAP = 64
HALO = 32
FP = 32
DEVICES = 128
MESH = pl.DeviceIdType.MESH
NT = (((1,), (1,)), ((), ()))


def target(step):
    y = lax.axis_index("expo")
    f = lax.axis_index("fp")
    a, b, c = lax.rem(step // 2, 4), lax.rem(step // 8, 4), step // 32
    ty = lax.rem(y + a + c, 4)
    tx = lax.rem(f // 8 + a + b, 4)
    tz = lax.rem(lax.rem(f // 2, 4) + a + b + c, 4)
    tc = lax.rem(f + step, 2)
    return ty, tx * 8 + tz * 2 + tc


def route_kernel(inv_ref, gap_ref, tile_ref, off_ref, src_ref, meta_ref):
    segs, rows = tile_ref.shape
    inv = inv_ref[0, 0]
    gap = gap_ref[0, 0]
    before = lax.broadcasted_iota(jnp.int32, (rows, rows), 0)
    after = lax.broadcasted_iota(jnp.int32, (rows, rows), 1)
    upper = (before < after).astype(jnp.float32).astype(jnp.bfloat16)
    tile_iota = lax.broadcasted_iota(jnp.int32, (DEVICES, rows), 0)
    slot_iota = lax.broadcasted_iota(jnp.int32, (CAP, rows), 0)
    row = lax.broadcasted_iota(jnp.int32, (1, rows), 1)
    open_row = jnp.where((row >= gap) & (row < gap + GAP), 0.0, 1.0)
    row_f = row.astype(jnp.float32)
    base = jnp.zeros((DEVICES, 1), jnp.float32)
    found = jnp.zeros((DEVICES, 5 * CAP), jnp.float32)
    for s in range(segs):
        hot = (tile_iota == tile_ref[s : s + 1, :]).astype(jnp.float32)
        hot_b = hot.astype(jnp.bfloat16)
        inside = jnp.dot(hot_b, upper, preferred_element_type=jnp.float32)
        rank = jnp.sum(hot * (inside + base), axis=0, keepdims=True)
        base = base + jnp.sum(hot, axis=1, keepdims=True)
        at_slot = (slot_iota == rank.astype(jnp.int32)).astype(jnp.float32)
        offset = off_ref[s : s + 1, :] + 1
        packed = jnp.concatenate(
            [
                at_slot * float(s),
                at_slot * row_f,
                at_slot * (offset >> 6).astype(jnp.float32),
                at_slot * (offset & 63).astype(jnp.float32),
                at_slot * open_row,
            ],
            axis=0,
        ).astype(jnp.bfloat16)
        found = found + lax.dot_general(hot_b, packed, NT, preferred_element_type=jnp.float32)
    source = found[:, :CAP] * float(rows) + found[:, CAP : 2 * CAP]
    src_ref[...] = source.astype(jnp.int32)
    offset = found[:, 2 * CAP : 3 * CAP] * 64.0 + found[:, 3 * CAP : 4 * CAP] - 1.0
    meta_ref[:, 0, :] = jnp.concatenate([offset, found[:, 4 * CAP :] * inv], axis=1)


def band(taps, rows, width, shift):
    wide = jnp.broadcast_to(taps[:, :width], (rows, width))
    return pltpu.roll(wide, shift - 4, 1, stride=1, stride_axis=0).astype(jnp.bfloat16)


def conv_kernel(
    id_ref, inv_ref, gap_ref, src_ref, bank_ref, up_ref, raw_ref, down_ref, send_ref,
    framed, vertical, pieces, stage,
):
    rows, cols = raw_ref.shape
    half = SEG
    kernel_id = id_ref[0, 0]
    vtap = bank_ref[pl.ds(2 * kernel_id, 1), :]
    htap = bank_ref[pl.ds(2 * kernel_id + 1, 1), :]
    framed[0:32, :] = jnp.zeros((32, cols), jnp.bfloat16)
    framed[32:64, :] = up_ref[...]
    framed[64 : 64 + rows, :] = raw_ref[...]
    framed[64 + rows : 96 + rows, :] = down_ref[...]
    framed[96 + rows : 128 + rows, :] = jnp.zeros((32, cols), jnp.bfloat16)
    vertical[:, :SEG] = jnp.zeros((rows, SEG), jnp.bfloat16)
    vertical[:, SEG + cols :] = jnp.zeros((rows, SEG), jnp.bfloat16)
    vband = band(vtap, half, 256, 44)
    hband = band(htap, 256, 512, 108)
    for n in range(cols // 512):
        for m in range(rows // half):
            made = jnp.dot(
                vband,
                framed[m * half : m * half + 256, n * 512 : (n + 1) * 512],
                preferred_element_type=jnp.float32,
            )
            vertical[m * half : (m + 1) * half, SEG + n * 512 : SEG + (n + 1) * 512] = made.astype(
                jnp.bfloat16
            )
    row = lax.broadcasted_iota(jnp.int32, (rows, 256), 0)
    gap = gap_ref[0, 0]
    weight = jnp.where((row >= gap) & (row < gap + GAP), 0.0, inv_ref[0, 0])
    for n in range(cols // 256):
        made = lax.dot_general(
            vertical[:, n * 256 : n * 256 + 512], hband, NT, preferred_element_type=jnp.float32
        )
        made = made.astype(jnp.bfloat16).astype(jnp.float32) * weight
        pieces[2 * n * rows : (2 * n + 1) * rows, :] = made[:, :SEG]
        pieces[(2 * n + 1) * rows : (2 * n + 2) * rows, :] = made[:, SEG:]

    def pack(pair, carry):
        for side in range(2):
            for k in range(CAP):
                stage[side, k : k + 1, :] = pieces[pl.ds(src_ref[2 * pair + side, k], 1), :]
        for side in range(2):
            send_ref[2 * pair + side] = stage[side].astype(jnp.bfloat16)
        return carry

    lax.fori_loop(0, DEVICES // 2, pack, 0)


def exchange_kernel(send_ref, meta_ref, got_ref, gmeta_ref, vsend, vrecv, msend, mrecv, local):
    barrier = pltpu.get_barrier_semaphore()

    def greet(step, carry):
        pl.semaphore_signal(barrier, inc=1, device_id=target(step), device_id_type=MESH)
        return carry

    lax.fori_loop(1, DEVICES, greet, 0)
    me = lax.axis_index("expo") * FP + lax.axis_index("fp")
    own = pltpu.make_async_copy(send_ref.at[me], got_ref.at[0], local.at[0])
    own.start()
    own_meta = pltpu.make_async_copy(meta_ref.at[me], gmeta_ref.at[0], local.at[1])
    own_meta.start()
    pl.semaphore_wait(barrier, DEVICES - 1)

    def copies(step):
        ty, tf = target(step)
        to = ty * FP + tf
        return (
            pltpu.make_async_remote_copy(
                src_ref=meta_ref.at[to], dst_ref=gmeta_ref.at[step],
                send_sem=msend.at[step], recv_sem=mrecv.at[step],
                device_id=(ty, tf), device_id_type=MESH,
            ),
            pltpu.make_async_remote_copy(
                src_ref=send_ref.at[to], dst_ref=got_ref.at[step],
                send_sem=vsend.at[step], recv_sem=vrecv.at[step],
                device_id=(ty, tf), device_id_type=MESH,
            ),
        )

    def start(step, carry):
        for copy in copies(step):
            copy.start()
        return carry

    def finish(step, carry):
        for copy in copies(step):
            copy.wait()
        return carry

    lax.fori_loop(1, DEVICES, start, 0)
    lax.fori_loop(1, DEVICES, finish, 0)
    own.wait()
    own_meta.wait()


PARTS = 8
SPAN = 512
GROUP = 8


def coadd_kernel(got_ref, gmeta_ref, image_ref, weight_ref, total):
    span_iota = lax.broadcasted_iota(jnp.int32, (SPAN, GROUP * CAP), 0)
    lane = lax.broadcasted_iota(jnp.int32, (GROUP * CAP, SEG), 1)
    total[...] = jnp.zeros_like(total)

    def chunk(j, carry):
        meta = gmeta_ref[pl.ds(j * GROUP, GROUP), 0, :]
        slots = jnp.concatenate([meta[i : i + 1, :CAP] for i in range(GROUP)], axis=1)
        slots = slots.astype(jnp.int32) & (SPAN - 1)
        hot = (span_iota == slots).astype(jnp.float32).astype(jnp.bfloat16)
        turned = meta.T
        column = jnp.concatenate([turned[:CAP, i : i + 1] for i in range(GROUP)], axis=0)
        part = jnp.broadcast_to(column, (GROUP * CAP, SEG)).astype(jnp.int32) >> 9
        weight = jnp.concatenate([turned[CAP:, i : i + 1] for i in range(GROUP)], axis=0)
        weight = jnp.broadcast_to(weight, (GROUP * CAP, SEG))
        high = weight.astype(jnp.bfloat16).astype(jnp.float32)
        spread = jnp.where(lane == part, high, 0.0)
        spread = spread + jnp.where(lane == part + PARTS, jnp.where(part < 0, 0.0, weight - high), 0.0)
        values = got_ref[pl.ds(j * GROUP, GROUP)].reshape(GROUP * CAP, SEG)
        values = values.astype(jnp.float32)
        masked = [jnp.where(part == a, values, 0.0).astype(jnp.bfloat16) for a in range(PARTS)]
        right = jnp.concatenate(masked + [spread.astype(jnp.bfloat16)], axis=1)
        total[...] += jnp.dot(hot, right, preferred_element_type=jnp.float32)
        return carry

    lax.fori_loop(0, DEVICES // GROUP, chunk, 0)
    sums = total[:, PARTS * SEG :]
    sums = sums[:, :PARTS] + sums[:, PARTS : 2 * PARTS]
    for a in range(PARTS):
        divisor = jnp.maximum(sums[:, a : a + 1], 1.0)
        image_ref[a * SPAN : (a + 1) * SPAN, :] = total[:, a * SEG : (a + 1) * SEG] / divisor
    turned = sums.T
    for a in range(PARTS):
        weight_ref[:, a * SPAN : (a + 1) * SPAN] = turned[a : a + 1, :]


def body(raw_pixels, kernel_bank, kernel_ids, inv_var, gap_start, warp_tile, warp_offset):
    raw = raw_pixels[0]
    rows, cols = raw.shape
    up = [(i, i + 1) for i in range(FP - 1)]
    down = [(i + 1, i) for i in range(FP - 1)]
    above = lax.ppermute(raw[rows - HALO :], "fp", up)
    below = lax.ppermute(raw[:HALO], "fp", down)
    bank = kernel_bank.astype(jnp.float32).reshape(-1, kernel_bank.shape[2])
    bank = jnp.pad(bank, ((0, 0), (4, 508 - bank.shape[1])))
    tiles = warp_tile[0, :, :, 0].T
    offsets = warp_offset[0].T
    smem = pl.BlockSpec(memory_space=pltpu.SMEM)
    vmem = pl.BlockSpec(memory_space=pltpu.VMEM)
    hbm = pl.BlockSpec(memory_space=pl.ANY)
    source, meta = pl.pallas_call(
        route_kernel,
        out_shape=(
            jax.ShapeDtypeStruct((DEVICES, CAP), jnp.int32),
            jax.ShapeDtypeStruct((DEVICES, 1, 2 * CAP), jnp.float32),
        ),
        in_specs=[smem, smem, vmem, vmem],
        out_specs=(vmem, vmem),
        cost_estimate=pl.CostEstimate(flops=10**9, bytes_accessed=10**6, transcendentals=0),
        name="route",
    )(inv_var, gap_start, tiles, offsets)
    send = pl.pallas_call(
        conv_kernel,
        out_shape=jax.ShapeDtypeStruct((DEVICES, CAP, SEG), jnp.bfloat16),
        in_specs=[smem, smem, smem, smem, vmem, vmem, vmem, vmem],
        out_specs=vmem,
        scratch_shapes=[
            pltpu.VMEM((rows + 128, cols), jnp.bfloat16),
            pltpu.VMEM((rows, cols + 2 * SEG), jnp.bfloat16),
            pltpu.VMEM((rows * cols // SEG, SEG), jnp.float32),
            pltpu.VMEM((2, CAP, SEG), jnp.float32),
        ],
        compiler_params=pltpu.CompilerParams(vmem_limit_bytes=40 << 20),
        name="conv_pack",
    )(kernel_ids, inv_var, gap_start, source, bank, above, raw, below)
    got, gmeta = pl.pallas_call(
        exchange_kernel,
        out_shape=(
            jax.ShapeDtypeStruct(send.shape, send.dtype),
            jax.ShapeDtypeStruct(meta.shape, meta.dtype),
        ),
        in_specs=[hbm, hbm],
        out_specs=(hbm, hbm),
        scratch_shapes=[pltpu.SemaphoreType.DMA((DEVICES,))] * 4 + [pltpu.SemaphoreType.DMA((2,))],
        compiler_params=pltpu.CompilerParams(collective_id=0, has_side_effects=True),
        name="exchange",
    )(send, meta)
    image, weight = pl.pallas_call(
        coadd_kernel,
        out_shape=(
            jax.ShapeDtypeStruct((PARTS * SPAN, SEG), jnp.float32),
            jax.ShapeDtypeStruct((1, PARTS * SPAN), jnp.float32),
        ),
        in_specs=[vmem, vmem],
        out_specs=(vmem, vmem),
        scratch_shapes=[pltpu.VMEM((SPAN, (PARTS + 1) * SEG), jnp.float32)],
        compiler_params=pltpu.CompilerParams(vmem_limit_bytes=40 << 20),
        name="coadd",
    )(got, gmeta)
    return image[None], weight


def solution(mesh):
    in_specs = (
        P("expo", "fp", None),
        P(),
        P("expo", "fp"),
        P("expo", "fp"),
        P("expo", "fp"),
        P("expo", "fp", None, None),
        P("expo", "fp", None),
    )
    out_specs = (P(("expo", "fp"), None, None), P(("expo", "fp"), None))
    return jax.shard_map(body, mesh=mesh, in_specs=in_specs, out_specs=out_specs, check_vma=False)
```

```python
import jax
import jax.numpy as jnp
from jax import lax
from jax.experimental import pallas as pl
from jax.experimental.pallas import tpu as pltpu
from jax.sharding import PartitionSpec as P

GAP = 32
SEG = 128
CAP = 64
HALO = 32
FP = 32
DEVICES = 128
MESH = pl.DeviceIdType.MESH
NT = (((1,), (1,)), ((), ()))


def corner(group):
    y = lax.axis_index("expo")
    f = lax.axis_index("fp")
    b, c = lax.rem(group, 4), group // 4
    return y + c, f // 8 + b, lax.rem(f // 2, 4) + b + c, lax.rem(f, 2)


def target(at, i):
    y, x, z, core = at
    a = i // 2
    ty = lax.rem(y + a, 4)
    tf = lax.rem(x + a, 4) * 8 + lax.rem(z + a, 4) * 2 + lax.rem(core + i, 2)
    return ty, tf


def front_kernel(
    id_ref, inv_ref, gap_ref, bank_ref, tile_ref, off_ref, raw_ref,
    src_ref, meta_ref, taps_ref, up_ref, down_ref, send_sem, recv_sem,
):
    y = lax.axis_index("expo")
    f = lax.axis_index("fp")
    top = raw_ref.shape[0] - HALO
    barrier = pltpu.get_barrier_semaphore()
    to_next = pltpu.make_async_remote_copy(
        src_ref=raw_ref.at[pl.ds(top, HALO)], dst_ref=up_ref,
        send_sem=send_sem.at[0], recv_sem=recv_sem.at[0],
        device_id=(y, f + 1), device_id_type=MESH,
    )
    to_last = pltpu.make_async_remote_copy(
        src_ref=raw_ref.at[pl.ds(0, HALO)], dst_ref=down_ref,
        send_sem=send_sem.at[1], recv_sem=recv_sem.at[1],
        device_id=(y, f - 1), device_id_type=MESH,
    )

    @pl.when(f > 0)
    def _():
        pl.semaphore_signal(barrier, inc=1, device_id=(y, f - 1), device_id_type=MESH)

    @pl.when(f < FP - 1)
    def _():
        pl.semaphore_signal(barrier, inc=1, device_id=(y, f + 1), device_id_type=MESH)

    @pl.when(f == 0)
    def _():
        up_ref[...] = jnp.zeros_like(up_ref)

    @pl.when(f == FP - 1)
    def _():
        down_ref[...] = jnp.zeros_like(down_ref)

    taps_ref[...] = jnp.zeros_like(taps_ref)
    taps_ref[0:2, 4 : 4 + bank_ref.shape[2]] = bank_ref[id_ref[0, 0]].astype(jnp.float32)

    inner = (f > 0) & (f < FP - 1)

    @pl.when(inner)
    def _():
        pl.semaphore_wait(barrier, 2)

    @pl.when(jnp.logical_not(inner))
    def _():
        pl.semaphore_wait(barrier, 1)

    @pl.when(f < FP - 1)
    def _():
        to_next.start()

    @pl.when(f > 0)
    def _():
        to_last.start()

    route(inv_ref, gap_ref, tile_ref, off_ref, src_ref, meta_ref)

    @pl.when(f < FP - 1)
    def _():
        to_next.wait_send()
        to_last.wait_recv()

    @pl.when(f > 0)
    def _():
        to_last.wait_send()
        to_next.wait_recv()


def route(inv_ref, gap_ref, tile_ref, off_ref, src_ref, meta_ref):
    segs, _, rows = tile_ref.shape
    inv = inv_ref[0, 0]
    gap = gap_ref[0, 0]
    before = lax.broadcasted_iota(jnp.int32, (rows, rows), 0)
    after = lax.broadcasted_iota(jnp.int32, (rows, rows), 1)
    upper = (before < after).astype(jnp.float32).astype(jnp.bfloat16)
    tile_iota = lax.broadcasted_iota(jnp.int32, (DEVICES, rows), 0)
    slot_iota = lax.broadcasted_iota(jnp.int32, (CAP, rows), 0)
    row = lax.broadcasted_iota(jnp.int32, (1, rows), 1)
    open_row = jnp.where((row >= gap) & (row < gap + GAP), 0.0, 1.0)
    row_f = row.astype(jnp.float32)
    base = jnp.zeros((DEVICES, 1), jnp.float32)
    found = jnp.zeros((DEVICES, 5 * CAP), jnp.float32)
    for s in range(segs):
        hot = (tile_iota == tile_ref[s]).astype(jnp.float32)
        hot_b = hot.astype(jnp.bfloat16)
        inside = jnp.dot(hot_b, upper, preferred_element_type=jnp.float32)
        rank = jnp.sum(hot * (inside + base), axis=0, keepdims=True)
        base = base + jnp.sum(hot, axis=1, keepdims=True)
        at_slot = (slot_iota == rank.astype(jnp.int32)).astype(jnp.float32)
        offset = off_ref[s : s + 1, :] + 1
        packed = jnp.concatenate(
            [
                at_slot * float(s),
                at_slot * row_f,
                at_slot * (offset >> 6).astype(jnp.float32),
                at_slot * (offset & 63).astype(jnp.float32),
                at_slot * open_row,
            ],
            axis=0,
        ).astype(jnp.bfloat16)
        found = found + lax.dot_general(hot_b, packed, NT, preferred_element_type=jnp.float32)
    source = found[:, :CAP] * float(rows) + found[:, CAP : 2 * CAP]
    src_ref[...] = source.astype(jnp.int32)
    offset = found[:, 2 * CAP : 3 * CAP] * 64.0 + found[:, 3 * CAP : 4 * CAP] - 1.0
    meta_ref[:, 0, :] = jnp.concatenate([offset, found[:, 4 * CAP :] * inv], axis=1)


def band(taps, rows, width, shift):
    wide = jnp.broadcast_to(taps[:, :width], (rows, width))
    return pltpu.roll(wide, shift - 4, 1, stride=1, stride_axis=0).astype(jnp.bfloat16)


PARTS = 8
SPAN = 512
GROUP = 8


def fused_kernel(
    inv_ref, gap_ref, src_ref, taps_ref, up_ref, raw_ref, down_ref, meta_ref, total,
    framed, vertical, pieces, stage, sent, got, gmeta, vsend, vrecv, msend, mrecv, local,
):
    barrier = pltpu.get_barrier_semaphore()
    groups = DEVICES // GROUP

    def greet(j, carry):
        at = corner(j)
        for i in range(GROUP):
            if i:
                pl.semaphore_signal(barrier, inc=1, device_id=target(at, i), device_id_type=MESH)
            else:

                @pl.when(j > 0)
                def _():
                    pl.semaphore_signal(
                        barrier, inc=1, device_id=target(at, 0), device_id_type=MESH
                    )

        return carry

    lax.fori_loop(0, groups, greet, 0)
    rows, cols = raw_ref.shape
    half = SEG
    vtap = taps_ref[0:1, :]
    htap = taps_ref[1:2, :]
    framed[0:32, :] = jnp.zeros((32, cols), jnp.bfloat16)
    framed[32:64, :] = up_ref[...]
    framed[64 : 64 + rows, :] = raw_ref[...]
    framed[64 + rows : 96 + rows, :] = down_ref[...]
    framed[96 + rows : 128 + rows, :] = jnp.zeros((32, cols), jnp.bfloat16)
    vertical[:, :SEG] = jnp.zeros((rows, SEG), jnp.bfloat16)
    vertical[:, SEG + cols :] = jnp.zeros((rows, SEG), jnp.bfloat16)
    vband = band(vtap, half, 256, 44)
    hband = band(htap, 256, 512, 108)
    for n in range(cols // 512):
        for m in range(rows // half):
            made = jnp.dot(
                vband,
                framed[m * half : m * half + 256, n * 512 : (n + 1) * 512],
                preferred_element_type=jnp.float32,
            )
            vertical[m * half : (m + 1) * half, SEG + n * 512 : SEG + (n + 1) * 512] = made.astype(
                jnp.bfloat16
            )
    row = lax.broadcasted_iota(jnp.int32, (rows, 256), 0)
    gap = gap_ref[0, 0]
    weight = jnp.where((row >= gap) & (row < gap + GAP), 0.0, inv_ref[0, 0])
    for n in range(cols // 256):
        made = lax.dot_general(
            vertical[:, n * 256 : n * 256 + 512], hband, NT, preferred_element_type=jnp.float32
        )
        made = made.astype(jnp.bfloat16).astype(jnp.float32) * weight
        pieces[2 * n * rows : (2 * n + 1) * rows, :] = made[:, :SEG]
        pieces[(2 * n + 1) * rows : (2 * n + 2) * rows, :] = made[:, SEG:]

    def copies(j, i, at):
        step = j * GROUP + i
        ty, tf = target(at, i)
        return (
            pltpu.make_async_remote_copy(
                src_ref=meta_ref.at[ty * FP + tf], dst_ref=gmeta.at[step],
                send_sem=msend.at[step], recv_sem=mrecv.at[step],
                device_id=(ty, tf), device_id_type=MESH,
            ),
            pltpu.make_async_remote_copy(
                src_ref=sent.at[step], dst_ref=got.at[step],
                send_sem=vsend.at[step], recv_sem=vrecv.at[step],
                device_id=(ty, tf), device_id_type=MESH,
            ),
        )

    me = lax.axis_index("expo") * FP + lax.axis_index("fp")
    own_meta = pltpu.make_async_copy(meta_ref.at[me], gmeta.at[0], local.at[0])
    own = pltpu.make_async_copy(sent.at[0], got.at[0], local.at[1])
    pl.semaphore_wait(barrier, DEVICES - 1)

    def pack(j, carry):
        at = corner(j)
        for i in range(GROUP):
            ty, tf = target(at, i)
            to = ty * FP + tf
            for k in range(CAP):
                stage[i, k : k + 1, :] = pieces[pl.ds(src_ref[to, k], 1), :]
            sent[j * GROUP + i] = stage[i].astype(jnp.bfloat16)
            if i:
                for copy in copies(j, i, at):
                    copy.start()
            else:

                @pl.when(j > 0)
                def _():
                    for copy in copies(j, 0, at):
                        copy.start()

                @pl.when(j == 0)
                def _():
                    own_meta.start()
                    own.start()

        return carry

    lax.fori_loop(0, groups, pack, 0)
    span_iota = lax.broadcasted_iota(jnp.int32, (SPAN, GROUP * CAP), 0)
    lane = lax.broadcasted_iota(jnp.int32, (GROUP * CAP, SEG), 1)
    total[...] = jnp.zeros_like(total)

    def chunk(j, carry):
        at = corner(j)
        for i in range(GROUP):
            if i:
                for copy in copies(j, i, at):
                    copy.wait_recv()
            else:

                @pl.when(j > 0)
                def _():
                    for copy in copies(j, 0, at):
                        copy.wait_recv()

                @pl.when(j == 0)
                def _():
                    own_meta.wait()
                    own.wait()

        meta = gmeta[pl.ds(j * GROUP, GROUP), 0, :]
        slots = jnp.concatenate([meta[i : i + 1, :CAP] for i in range(GROUP)], axis=1)
        slots = slots.astype(jnp.int32) & (SPAN - 1)
        hot = (span_iota == slots).astype(jnp.float32).astype(jnp.bfloat16)
        turned = meta.T
        column = jnp.concatenate([turned[:CAP, i : i + 1] for i in range(GROUP)], axis=0)
        part = jnp.broadcast_to(column, (GROUP * CAP, SEG)).astype(jnp.int32) >> 9
        weight = jnp.concatenate([turned[CAP:, i : i + 1] for i in range(GROUP)], axis=0)
        weight = jnp.broadcast_to(weight, (GROUP * CAP, SEG))
        high = weight.astype(jnp.bfloat16).astype(jnp.float32)
        spread = jnp.where(lane == part, high, 0.0)
        spread = spread + jnp.where(lane == part + PARTS, jnp.where(part < 0, 0.0, weight - high), 0.0)
        values = got[pl.ds(j * GROUP, GROUP)].reshape(GROUP * CAP, SEG)
        values = values.astype(jnp.float32)
        masked = [jnp.where(part == a, values, 0.0).astype(jnp.bfloat16) for a in range(PARTS)]
        right = jnp.concatenate(masked + [spread.astype(jnp.bfloat16)], axis=1)
        total[...] += jnp.dot(hot, right, preferred_element_type=jnp.float32)
        return carry

    lax.fori_loop(0, groups, chunk, 0)

    def finish(j, carry):
        at = corner(j)
        for i in range(GROUP):
            if i:
                for copy in copies(j, i, at):
                    copy.wait_send()
            else:

                @pl.when(j > 0)
                def _():
                    for copy in copies(j, 0, at):
                        copy.wait_send()

        return carry

    lax.fori_loop(0, groups, finish, 0)


def mean_kernel(total_ref, image_ref, weight_ref, mean, sems):
    sums = total_ref[:, PARTS * SEG :]
    sums = sums[:, :PARTS] + sums[:, PARTS : 2 * PARTS]
    scale = 1.0 / jnp.maximum(sums, 1.0)
    copies = []
    for a in range(PARTS):
        slots = slice(a * SPAN, (a + 1) * SPAN)
        mean[slots, :] = total_ref[:, a * SEG : (a + 1) * SEG] * scale[:, a : a + 1]
        copies.append(
            pltpu.make_async_copy(
                mean.at[pl.ds(a * SPAN, SPAN)], image_ref.at[pl.ds(a * SPAN, SPAN)], sems.at[a]
            )
        )
        copies[-1].start()
    turned = sums.T
    for a in range(PARTS):
        weight_ref[:, a * SPAN : (a + 1) * SPAN] = turned[a : a + 1, :]
    for copy in copies:
        copy.wait()


def body(raw_pixels, kernel_bank, kernel_ids, inv_var, gap_start, warp_tile, warp_offset):
    raw = raw_pixels[0]
    rows, cols = raw.shape
    tiles = jnp.transpose(warp_tile[0], (1, 2, 0))
    offsets = warp_offset[0].T
    smem = pl.BlockSpec(memory_space=pltpu.SMEM)
    vmem = pl.BlockSpec(memory_space=pltpu.VMEM)
    hbm = pl.BlockSpec(memory_space=pl.ANY)
    dma = pltpu.SemaphoreType.DMA
    source, meta, taps, above, below = pl.pallas_call(
        front_kernel,
        out_shape=(
            jax.ShapeDtypeStruct((DEVICES, CAP), jnp.int32),
            jax.ShapeDtypeStruct((DEVICES, 1, 2 * CAP), jnp.float32),
            jax.ShapeDtypeStruct((8, 512), jnp.float32),
            jax.ShapeDtypeStruct((HALO, cols), jnp.bfloat16),
            jax.ShapeDtypeStruct((HALO, cols), jnp.bfloat16),
        ),
        in_specs=[smem, smem, smem, vmem, vmem, vmem, hbm],
        out_specs=(vmem,) * 5,
        scratch_shapes=[dma((2,)), dma((2,))],
        compiler_params=pltpu.CompilerParams(
            collective_id=0, has_side_effects=True, vmem_limit_bytes=16 << 20
        ),
        name="front",
    )(kernel_ids, inv_var, gap_start, kernel_bank, tiles, offsets, raw)
    total = pl.pallas_call(
        fused_kernel,
        out_shape=jax.ShapeDtypeStruct((SPAN, (PARTS + 1) * SEG), jnp.float32),
        in_specs=[smem, smem, smem] + [vmem] * 5,
        out_specs=vmem,
        scratch_shapes=[
            pltpu.VMEM((rows + 128, cols), jnp.bfloat16),
            pltpu.VMEM((rows, cols + 2 * SEG), jnp.bfloat16),
            pltpu.VMEM((rows * cols // SEG, SEG), jnp.float32),
            pltpu.VMEM((GROUP, CAP, SEG), jnp.float32),
            pltpu.VMEM((DEVICES, CAP, SEG), jnp.bfloat16),
            pltpu.VMEM((DEVICES, CAP, SEG), jnp.bfloat16),
            pltpu.VMEM((DEVICES, 1, 2 * CAP), jnp.float32),
            dma((DEVICES,)), dma((DEVICES,)), dma((DEVICES,)), dma((DEVICES,)), dma((2,)),
        ],
        compiler_params=pltpu.CompilerParams(
            collective_id=1, has_side_effects=True, vmem_limit_bytes=40 << 20
        ),
        name="fused",
    )(inv_var, gap_start, source, taps, above, raw, below, meta)
    image, weight = pl.pallas_call(
        mean_kernel,
        out_shape=(
            jax.ShapeDtypeStruct((PARTS * SPAN, SEG), jnp.float32),
            jax.ShapeDtypeStruct((1, PARTS * SPAN), jnp.float32),
        ),
        in_specs=[vmem],
        out_specs=(hbm, vmem),
        scratch_shapes=[pltpu.VMEM((PARTS * SPAN, SEG), jnp.float32), dma((PARTS,))],
        compiler_params=pltpu.CompilerParams(vmem_limit_bytes=16 << 20),
        name="mean",
    )(total)
    return image[None], weight


def solution(mesh):
    in_specs = (
        P("expo", "fp", None),
        P(),
        P("expo", "fp"),
        P("expo", "fp"),
        P("expo", "fp"),
        P("expo", "fp", None, None),
        P("expo", "fp", None),
    )
    out_specs = (P(("expo", "fp"), None, None), P(("expo", "fp"), None))
    return jax.shard_map(body, mesh=mesh, in_specs=in_specs, out_specs=out_specs, check_vma=False)
```

```python
import jax
import jax.numpy as jnp
from jax import lax
from jax.experimental import pallas as pl
from jax.experimental.pallas import tpu as pltpu
from jax.sharding import PartitionSpec as P

GAP = 32
SEG = 128
CAP = 64
HALO = 32
FP = 32
DEVICES = 128
MESH = pl.DeviceIdType.MESH
NT = (((1,), (1,)), ((), ()))


def corner(group):
    y = lax.axis_index("expo")
    f = lax.axis_index("fp")
    b, c = lax.rem(group, 4), group // 4
    return y + c, f // 8 + b, lax.rem(f // 2, 4) + b + c, lax.rem(f, 2)


def target(at, i):
    y, x, z, core = at
    a = i // 2
    ty = lax.rem(y + a, 4)
    tf = lax.rem(x + a, 4) * 8 + lax.rem(z + a, 4) * 2 + lax.rem(core + i, 2)
    return ty, tf


def front_kernel(
    id_ref, inv_ref, gap_ref, bank_hbm, tile_hbm, off_hbm, raw_ref,
    src_ref, meta_ref, taps_ref, up_ref, down_ref, send_sem, recv_sem,
    bank_ref, tile_ref, off_ref, load_sem,
):
    y = lax.axis_index("expo")
    f = lax.axis_index("fp")
    top = raw_ref.shape[0] - HALO
    loads = [
        pltpu.make_async_copy(source, ref, load_sem.at[n])
        for n, (source, ref) in enumerate(
            [(bank_hbm, bank_ref), (tile_hbm, tile_ref), (off_hbm, off_ref)]
        )
    ]
    for load in loads:
        load.start()
    barrier = pltpu.get_barrier_semaphore()
    to_next = pltpu.make_async_remote_copy(
        src_ref=raw_ref.at[pl.ds(top, HALO)], dst_ref=up_ref,
        send_sem=send_sem.at[0], recv_sem=recv_sem.at[0],
        device_id=(y, f + 1), device_id_type=MESH,
    )
    to_last = pltpu.make_async_remote_copy(
        src_ref=raw_ref.at[pl.ds(0, HALO)], dst_ref=down_ref,
        send_sem=send_sem.at[1], recv_sem=recv_sem.at[1],
        device_id=(y, f - 1), device_id_type=MESH,
    )

    @pl.when(f > 0)
    def _():
        pl.semaphore_signal(barrier, inc=1, device_id=(y, f - 1), device_id_type=MESH)

    @pl.when(f < FP - 1)
    def _():
        pl.semaphore_signal(barrier, inc=1, device_id=(y, f + 1), device_id_type=MESH)

    @pl.when(f == 0)
    def _():
        up_ref[...] = jnp.zeros_like(up_ref)

    @pl.when(f == FP - 1)
    def _():
        down_ref[...] = jnp.zeros_like(down_ref)

    for load in loads:
        load.wait()
    taps_ref[...] = jnp.zeros_like(taps_ref)
    taps_ref[0:2, 4 : 4 + bank_ref.shape[2]] = bank_ref[id_ref[0, 0]].astype(jnp.float32)

    inner = (f > 0) & (f < FP - 1)

    @pl.when(inner)
    def _():
        pl.semaphore_wait(barrier, 2)

    @pl.when(jnp.logical_not(inner))
    def _():
        pl.semaphore_wait(barrier, 1)

    @pl.when(f < FP - 1)
    def _():
        to_next.start()

    @pl.when(f > 0)
    def _():
        to_last.start()

    route(inv_ref, gap_ref, tile_ref, off_ref, src_ref, meta_ref)

    @pl.when(f < FP - 1)
    def _():
        to_next.wait_send()
        to_last.wait_recv()

    @pl.when(f > 0)
    def _():
        to_last.wait_send()
        to_next.wait_recv()


def route(inv_ref, gap_ref, tile_ref, off_ref, src_ref, meta_ref):
    segs, _, rows = tile_ref.shape
    inv = inv_ref[0, 0]
    gap = gap_ref[0, 0]
    before = lax.broadcasted_iota(jnp.int32, (rows, rows), 0)
    after = lax.broadcasted_iota(jnp.int32, (rows, rows), 1)
    upper = (before < after).astype(jnp.float32).astype(jnp.bfloat16)
    tile_iota = lax.broadcasted_iota(jnp.int32, (DEVICES, rows), 0)
    slot_iota = lax.broadcasted_iota(jnp.int32, (CAP, rows), 0)
    row = lax.broadcasted_iota(jnp.int32, (1, rows), 1)
    open_row = jnp.where((row >= gap) & (row < gap + GAP), 0.0, 1.0)
    row_f = row.astype(jnp.float32)
    base = jnp.zeros((DEVICES, 1), jnp.float32)
    found = jnp.zeros((DEVICES, 5 * CAP), jnp.float32)
    for s in range(segs):
        hot = (tile_iota == tile_ref[s]).astype(jnp.float32)
        hot_b = hot.astype(jnp.bfloat16)
        inside = jnp.dot(hot_b, upper, preferred_element_type=jnp.float32)
        rank = jnp.sum(hot * (inside + base), axis=0, keepdims=True)
        base = base + jnp.sum(hot, axis=1, keepdims=True)
        at_slot = (slot_iota == rank.astype(jnp.int32)).astype(jnp.float32)
        offset = off_ref[s : s + 1, :] + 1
        packed = jnp.concatenate(
            [
                at_slot * float(s),
                at_slot * row_f,
                at_slot * (offset >> 6).astype(jnp.float32),
                at_slot * (offset & 63).astype(jnp.float32),
                at_slot * open_row,
            ],
            axis=0,
        ).astype(jnp.bfloat16)
        found = found + lax.dot_general(hot_b, packed, NT, preferred_element_type=jnp.float32)
    source = found[:, :CAP] * float(rows) + found[:, CAP : 2 * CAP]
    src_ref[...] = source.astype(jnp.int32)
    offset = found[:, 2 * CAP : 3 * CAP] * 64.0 + found[:, 3 * CAP : 4 * CAP] - 1.0
    meta_ref[:, 0, :] = jnp.concatenate([offset, found[:, 4 * CAP :] * inv], axis=1)


def band(taps, rows, width, shift):
    wide = jnp.broadcast_to(taps[:, :width], (rows, width))
    return pltpu.roll(wide, shift - 4, 1, stride=1, stride_axis=0).astype(jnp.bfloat16)


PARTS = 8
SPAN = 512
GROUP = 8


def fused_kernel(
    inv_ref, gap_ref, src_ref, taps_ref, up_ref, raw_ref, down_ref, meta_ref, total, weights,
    framed, vertical, pieces, stage, sent, got, gmeta, vsend, vrecv, msend, mrecv, local,
):
    barrier = pltpu.get_barrier_semaphore()
    groups = DEVICES // GROUP

    y = lax.axis_index("expo")
    f = lax.axis_index("fp")
    ys = [lax.rem(y + k, 4) for k in range(4)]
    xs = [lax.rem(f // 8 + k, 4) * 8 for k in range(4)]
    zs = [lax.rem(f // 2 + k, 4) * 2 for k in range(4)]
    cores = [lax.rem(f + k, 2) for k in range(2)]
    for step in range(1, DEVICES):
        a, b, c = step // 2 % 4, step // 8 % 4, step // 32
        to = (ys[(a + c) % 4], xs[(a + b) % 4] + zs[(a + b + c) % 4] + cores[step % 2])
        pl.semaphore_signal(barrier, inc=1, device_id=to, device_id_type=MESH)
    rows, cols = raw_ref.shape
    half = SEG
    vtap = taps_ref[0:1, :]
    htap = taps_ref[1:2, :]
    framed[0:32, :] = jnp.zeros((32, cols), jnp.bfloat16)
    loads = [
        pltpu.make_async_copy(raw_ref, framed.at[pl.ds(64, rows)], local.at[2]),
        pltpu.make_async_copy(up_ref, framed.at[pl.ds(32, HALO)], local.at[3]),
        pltpu.make_async_copy(down_ref, framed.at[pl.ds(64 + rows, HALO)], local.at[4]),
    ]
    for load in loads:
        load.start()
    framed[96 + rows : 128 + rows, :] = jnp.zeros((32, cols), jnp.bfloat16)
    vertical[:, :SEG] = jnp.zeros((rows, SEG), jnp.bfloat16)
    vertical[:, SEG + cols :] = jnp.zeros((rows, SEG), jnp.bfloat16)
    vband = band(vtap, half, 256, 44)
    hband = band(htap, 256, 512, 108)
    for load in loads:
        load.wait()
    for n in range(cols // 512):
        for m in range(rows // half):
            made = jnp.dot(
                vband,
                framed[m * half : m * half + 256, n * 512 : (n + 1) * 512],
                preferred_element_type=jnp.float32,
            )
            vertical[m * half : (m + 1) * half, SEG + n * 512 : SEG + (n + 1) * 512] = made.astype(
                jnp.bfloat16
            )
    row = lax.broadcasted_iota(jnp.int32, (rows, 256), 0)
    gap = gap_ref[0, 0]
    weight = jnp.where((row >= gap) & (row < gap + GAP), 0.0, inv_ref[0, 0])
    for n in range(cols // 256):
        made = lax.dot_general(
            vertical[:, n * 256 : n * 256 + 512], hband, NT, preferred_element_type=jnp.float32
        )
        made = made.astype(jnp.bfloat16).astype(jnp.float32) * weight
        pieces[2 * n * rows : (2 * n + 1) * rows, :] = made[:, :SEG]
        pieces[(2 * n + 1) * rows : (2 * n + 2) * rows, :] = made[:, SEG:]

    def copies(j, i, at):
        step = j * GROUP + i
        ty, tf = target(at, i)
        return (
            pltpu.make_async_remote_copy(
                src_ref=meta_ref.at[ty * FP + tf], dst_ref=gmeta.at[step],
                send_sem=msend, recv_sem=mrecv.at[j],
                device_id=(ty, tf), device_id_type=MESH,
            ),
            pltpu.make_async_remote_copy(
                src_ref=sent.at[step], dst_ref=got.at[step],
                send_sem=vsend, recv_sem=vrecv.at[j],
                device_id=(ty, tf), device_id_type=MESH,
            ),
        )

    me = lax.axis_index("expo") * FP + lax.axis_index("fp")
    own_meta = pltpu.make_async_copy(meta_ref.at[me], gmeta.at[0], local.at[0])
    own = pltpu.make_async_copy(sent.at[0], got.at[0], local.at[1])
    pl.semaphore_wait(barrier, DEVICES - 1)

    def pack(j, carry):
        at = corner(j)
        for i in range(GROUP):
            ty, tf = target(at, i)
            to = ty * FP + tf
            for k in range(CAP):
                stage[i, k : k + 1, :] = pieces[pl.ds(src_ref[to, k], 1), :]
            sent[j * GROUP + i] = stage[i].astype(jnp.bfloat16)
            if i:
                for copy in copies(j, i, at):
                    copy.start()
            else:

                @pl.when(j > 0)
                def _():
                    for copy in copies(j, 0, at):
                        copy.start()

                @pl.when(j == 0)
                def _():
                    own_meta.start()
                    own.start()

        return carry

    lax.fori_loop(0, groups, pack, 0)
    span_iota = lax.broadcasted_iota(jnp.int32, (SPAN, GROUP * CAP), 0).astype(jnp.int16)
    part_iota = lax.broadcasted_iota(jnp.int32, (2 * PARTS, GROUP * CAP), 0)
    total[...] = jnp.zeros_like(total)
    weights[...] = jnp.zeros_like(weights)

    def arrived(j, first, count):
        for buffer, sem in ((gmeta, mrecv), (got, vrecv)):
            slots = buffer.at[pl.ds(j * GROUP + first, count)]
            pltpu.make_async_copy(slots, slots, sem.at[j]).wait()

    def chunk(j, carry):
        @pl.when(j > 0)
        def _():
            arrived(j, 0, GROUP)

        @pl.when(j == 0)
        def _():
            own_meta.wait()
            own.wait()
            arrived(0, 1, GROUP - 1)

        meta = gmeta[pl.ds(j * GROUP, GROUP), 0, :]
        slots = jnp.concatenate([meta[i : i + 1, :CAP] for i in range(GROUP)], axis=1)
        weight = jnp.concatenate([meta[i : i + 1, CAP:] for i in range(GROUP)], axis=1)
        slots = slots.astype(jnp.int32)
        inside = jnp.broadcast_to(slots & (SPAN - 1), (16, GROUP * CAP)).astype(jnp.int16)
        inside = jnp.broadcast_to(inside[:1], (SPAN, GROUP * CAP))
        hot = jnp.where(span_iota == inside, jnp.bfloat16(1), jnp.bfloat16(0))
        high = weight.astype(jnp.bfloat16).astype(jnp.float32)
        part = slots >> 9
        spread = jnp.where(part_iota == part, high, 0.0)
        spread = jnp.where((part_iota == part + PARTS) & (part >= 0), weight - high, spread)
        weights[...] += lax.dot_general(
            spread.astype(jnp.bfloat16), hot, NT, preferred_element_type=jnp.float32
        )
        turned = jnp.floor(meta * (1.0 / SPAN)).T
        column = jnp.concatenate([turned[:CAP, i : i + 1] for i in range(GROUP)], axis=0)
        part = jnp.broadcast_to(column, (GROUP * CAP, SEG)).astype(jnp.bfloat16)
        values = got[pl.ds(j * GROUP, GROUP)].reshape(GROUP * CAP, SEG)
        none = jnp.zeros_like(values)
        masked = [jnp.where(part == jnp.bfloat16(a), values, none) for a in range(PARTS)]
        right = jnp.concatenate(masked, axis=1)
        total[...] += jnp.dot(hot, right, preferred_element_type=jnp.float32)
        return carry

    lax.fori_loop(0, groups, chunk, 0)

    for buffer, sem in ((meta_ref, msend), (sent, vsend)):
        slots = buffer.at[pl.ds(1, DEVICES - 1)]
        pltpu.make_async_copy(slots, slots, sem).wait()


def mean_kernel(total_ref, sums_ref, image_ref, weight_ref, mean, sems):
    sums = sums_ref[:PARTS, :] + sums_ref[PARTS:, :]
    scale = (1.0 / jnp.maximum(sums, 1.0)).T
    copies = []
    for a in range(PARTS):
        slots = slice(a * SPAN, (a + 1) * SPAN)
        mean[slots, :] = total_ref[:, a * SEG : (a + 1) * SEG] * scale[:, a : a + 1]
        copies.append(
            pltpu.make_async_copy(
                mean.at[pl.ds(a * SPAN, SPAN)], image_ref.at[pl.ds(a * SPAN, SPAN)], sems.at[a]
            )
        )
        copies[-1].start()
    for a in range(PARTS):
        weight_ref[:, a * SPAN : (a + 1) * SPAN] = sums[a : a + 1, :]
    for copy in copies:
        copy.wait()


def body(raw_pixels, kernel_bank, kernel_ids, inv_var, gap_start, warp_tile, warp_offset):
    raw = raw_pixels[0]
    rows, cols = raw.shape
    tiles = jnp.transpose(warp_tile[0], (1, 2, 0))
    offsets = warp_offset[0].T
    smem = pl.BlockSpec(memory_space=pltpu.SMEM)
    vmem = pl.BlockSpec(memory_space=pltpu.VMEM)
    hbm = pl.BlockSpec(memory_space=pl.ANY)
    fixed = pl.BlockSpec(memory_space=pltpu.HBM)
    dma = pltpu.SemaphoreType.DMA
    source, meta, taps, above, below = pl.pallas_call(
        front_kernel,
        out_shape=(
            jax.ShapeDtypeStruct((DEVICES, CAP), jnp.int32),
            jax.ShapeDtypeStruct((DEVICES, 1, 2 * CAP), jnp.float32),
            jax.ShapeDtypeStruct((8, 512), jnp.float32),
            jax.ShapeDtypeStruct((HALO, cols), jnp.bfloat16),
            jax.ShapeDtypeStruct((HALO, cols), jnp.bfloat16),
        ),
        in_specs=[smem, smem, smem, fixed, fixed, fixed, fixed],
        out_specs=(vmem,) * 5,
        scratch_shapes=[
            dma((2,)), dma((2,)),
            pltpu.VMEM(kernel_bank.shape, kernel_bank.dtype),
            pltpu.VMEM(tiles.shape, tiles.dtype),
            pltpu.VMEM(offsets.shape, offsets.dtype),
            dma((3,)),
        ],
        compiler_params=pltpu.CompilerParams(
            collective_id=0, has_side_effects=True, vmem_limit_bytes=16 << 20
        ),
        name="front",
    )(kernel_ids, inv_var, gap_start, kernel_bank, tiles, offsets, raw)
    total, sums = pl.pallas_call(
        fused_kernel,
        out_shape=(
            jax.ShapeDtypeStruct((SPAN, PARTS * SEG), jnp.float32),
            jax.ShapeDtypeStruct((2 * PARTS, SPAN), jnp.float32),
        ),
        in_specs=[smem, smem, smem, vmem, hbm, fixed, hbm, vmem],
        out_specs=(vmem, vmem),
        scratch_shapes=[
            pltpu.VMEM((rows + 128, cols), jnp.bfloat16),
            pltpu.VMEM((rows, cols + 2 * SEG), jnp.bfloat16),
            pltpu.VMEM((rows * cols // SEG, SEG), jnp.float32),
            pltpu.VMEM((GROUP, CAP, SEG), jnp.float32),
            pltpu.VMEM((DEVICES, CAP, SEG), jnp.bfloat16),
            pltpu.VMEM((DEVICES, CAP, SEG), jnp.bfloat16),
            pltpu.VMEM((DEVICES, 1, 2 * CAP), jnp.float32),
            dma, dma((DEVICES // GROUP,)), dma, dma((DEVICES // GROUP,)), dma((5,)),
        ],
        compiler_params=pltpu.CompilerParams(
            collective_id=1, has_side_effects=True, vmem_limit_bytes=40 << 20
        ),
        name="fused",
    )(inv_var, gap_start, source, taps, above, raw, below, meta)
    image, weight = pl.pallas_call(
        mean_kernel,
        out_shape=(
            jax.ShapeDtypeStruct((PARTS * SPAN, SEG), jnp.float32),
            jax.ShapeDtypeStruct((1, PARTS * SPAN), jnp.float32),
        ),
        in_specs=[vmem, vmem],
        out_specs=(fixed, vmem),
        scratch_shapes=[pltpu.VMEM((PARTS * SPAN, SEG), jnp.float32), dma((PARTS,))],
        compiler_params=pltpu.CompilerParams(vmem_limit_bytes=16 << 20),
        name="mean",
    )(total, sums)
    return image[None], weight


def solution(mesh):
    in_specs = (
        P("expo", "fp", None),
        P(),
        P("expo", "fp"),
        P("expo", "fp"),
        P("expo", "fp"),
        P("expo", "fp", None, None),
        P("expo", "fp", None),
    )
    out_specs = (P(("expo", "fp"), None, None), P(("expo", "fp"), None))
    return jax.shard_map(body, mesh=mesh, in_specs=in_specs, out_specs=out_specs, check_vma=False)
```

```python
import jax
import jax.numpy as jnp
from jax import lax
from jax.experimental import pallas as pl
from jax.experimental.pallas import tpu as pltpu
from jax.sharding import PartitionSpec as P

GAP = 32
SEG = 128
CAP = 64
HALO = 32
FP = 32
DEVICES = 128
MESH = pl.DeviceIdType.MESH
NT = (((1,), (1,)), ((), ()))


def corner(group):
    y = lax.axis_index("expo")
    f = lax.axis_index("fp")
    b, c = lax.rem(group, 4), group // 4
    return y + c, f // 8 + b, lax.rem(f // 2, 4) + b + c, lax.rem(f, 2)


def target(at, i):
    y, x, z, core = at
    a = i // 2
    ty = lax.rem(y + a, 4)
    tf = lax.rem(x + a, 4) * 8 + lax.rem(z + a, 4) * 2 + lax.rem(core + i, 2)
    return ty, tf


def route(inv_ref, gap_ref, tile_ref, off_ref, src_ref, meta_ref):
    segs, _, rows = tile_ref.shape
    inv = inv_ref[0, 0]
    gap = gap_ref[0, 0]
    before = lax.broadcasted_iota(jnp.int32, (rows, rows), 0)
    after = lax.broadcasted_iota(jnp.int32, (rows, rows), 1)
    upper = (before < after).astype(jnp.float32).astype(jnp.bfloat16)
    tile_iota = lax.broadcasted_iota(jnp.int32, (DEVICES, rows), 0)
    slot_iota = lax.broadcasted_iota(jnp.int32, (CAP, rows), 0)
    row = lax.broadcasted_iota(jnp.int32, (1, rows), 1)
    open_row = jnp.where((row >= gap) & (row < gap + GAP), 0.0, 1.0)
    row_f = row.astype(jnp.float32)
    base = jnp.zeros((DEVICES, 1), jnp.float32)
    found = jnp.zeros((DEVICES, 5 * CAP), jnp.float32)
    for s in range(segs):
        hot = (tile_iota == tile_ref[s]).astype(jnp.float32)
        hot_b = hot.astype(jnp.bfloat16)
        inside = jnp.dot(hot_b, upper, preferred_element_type=jnp.float32)
        rank = jnp.sum(hot * (inside + base), axis=0, keepdims=True)
        base = base + jnp.sum(hot, axis=1, keepdims=True)
        at_slot = (slot_iota == rank.astype(jnp.int32)).astype(jnp.float32)
        offset = off_ref[s : s + 1, :] + 1
        packed = jnp.concatenate(
            [
                at_slot * float(s),
                at_slot * row_f,
                at_slot * (offset >> 6).astype(jnp.float32),
                at_slot * (offset & 63).astype(jnp.float32),
                at_slot * open_row,
            ],
            axis=0,
        ).astype(jnp.bfloat16)
        found = found + lax.dot_general(hot_b, packed, NT, preferred_element_type=jnp.float32)
    source = found[:, :CAP] * float(rows) + found[:, CAP : 2 * CAP]
    source = jnp.concatenate([source, jnp.zeros_like(source)], axis=1).astype(jnp.int32)
    src_ref[...] = jnp.clip(source, 0, segs * rows - 1)
    offset = found[:, 2 * CAP : 3 * CAP] * 64.0 + found[:, 3 * CAP : 4 * CAP] - 1.0
    meta_ref[:, 0, :] = jnp.concatenate([offset, found[:, 4 * CAP :] * inv], axis=1)


def band(taps, rows, width, shift):
    wide = jnp.broadcast_to(taps[:, :width], (rows, width))
    return pltpu.roll(wide, shift - 4, 1, stride=1, stride_axis=0).astype(jnp.bfloat16)


PARTS = 8
SPAN = 512
GROUP = 8
AHEAD = 5


def fused_kernel(
    id_ref, inv_ref, gap_ref, bank_hbm, tile_hbm, off_hbm, raw_ref, image_ref, weight_ref,
    total, weights,
    bank_ref, tile_ref, off_ref, taps_ref, slot_ref, src_ref, meta_ref, up_ref, down_ref,
    framed, vertical, pieces, stage, sent, got, gmeta,
    vsend, vrecv, msend, mrecv, edge_send, edge_recv, local, store,
):
    barrier = pltpu.get_barrier_semaphore()
    groups = DEVICES // GROUP

    y = lax.axis_index("expo")
    f = lax.axis_index("fp")
    rows, cols = raw_ref.shape
    half = SEG
    loads = [
        pltpu.make_async_copy(source, ref, local.at[n])
        for n, (source, ref) in enumerate(
            [
                (tile_hbm, tile_ref),
                (off_hbm, off_ref),
                (bank_hbm, bank_ref),
                (raw_ref, framed.at[pl.ds(64, rows)]),
            ]
        )
    ]
    for load in loads:
        load.start()
    ys = [lax.rem(y + k, 4) for k in range(4)]
    xs = [lax.rem(f // 8 + k, 4) * 8 for k in range(4)]
    zs = [lax.rem(f // 2 + k, 4) * 2 for k in range(4)]
    cores = [lax.rem(f + k, 2) for k in range(2)]
    others = []
    for step in range(1, DEVICES):
        a, b, c = step // 2 % 4, step // 8 % 4, step // 32
        to = (ys[(a + c) % 4], xs[(a + b) % 4] + zs[(a + b + c) % 4] + cores[step % 2])
        others.append(to)
        pl.semaphore_signal(barrier, inc=1, device_id=to, device_id_type=MESH)
    framed[0:64, :] = jnp.zeros((64, cols), jnp.bfloat16)
    framed[64 + rows : 128 + rows, :] = jnp.zeros((64, cols), jnp.bfloat16)
    for load in loads[:3]:
        load.wait()
    route(inv_ref, gap_ref, tile_ref, off_ref, slot_ref, meta_ref)
    to_scalars = pltpu.make_async_copy(slot_ref, src_ref, local.at[4])
    to_scalars.start()
    taps_ref[...] = jnp.zeros_like(taps_ref)
    taps_ref[0:2, 4 : 4 + bank_ref.shape[2]] = bank_ref[id_ref[0, 0]].astype(jnp.float32)
    vtap = taps_ref[0:1, :]
    htap = taps_ref[1:2, :]
    vertical[:, :SEG] = jnp.zeros((rows, SEG), jnp.bfloat16)
    vertical[:, SEG + cols :] = jnp.zeros((rows, SEG), jnp.bfloat16)
    vband = band(vtap, half, 256, 44)
    hband = band(htap, 256, 512, 108)
    loads[3].wait()
    for n in range(cols // 512):
        for m in range(rows // half):
            made = jnp.dot(
                vband,
                framed[m * half : m * half + 256, n * 512 : (n + 1) * 512],
                preferred_element_type=jnp.float32,
            )
            vertical[m * half : (m + 1) * half, SEG + n * 512 : SEG + (n + 1) * 512] = made.astype(
                jnp.bfloat16
            )
    row = lax.broadcasted_iota(jnp.int32, (rows, 256), 0)
    gap = gap_ref[0, 0]
    weight = jnp.where((row >= gap) & (row < gap + GAP), 0.0, inv_ref[0, 0])
    for n in range(cols // 256):
        made = lax.dot_general(
            vertical[:, n * 256 : n * 256 + 512], hband, NT, preferred_element_type=jnp.float32
        )
        made = made.astype(jnp.bfloat16).astype(jnp.float32) * weight
        pieces[2 * n * rows : (2 * n + 1) * rows, :] = made[:, :SEG]
        pieces[(2 * n + 1) * rows : (2 * n + 2) * rows, :] = made[:, SEG:]

    me = y * FP + f
    own_meta = pltpu.make_async_copy(meta_ref.at[me], gmeta.at[0], local.at[5])
    own = pltpu.make_async_copy(sent.at[0], got.at[0], local.at[6])
    own_meta.start()
    to_next = pltpu.make_async_remote_copy(
        src_ref=framed.at[pl.ds(32 + rows, HALO)], dst_ref=up_ref,
        send_sem=edge_send.at[0], recv_sem=edge_recv.at[0],
        device_id=(y, f + 1), device_id_type=MESH,
    )
    to_last = pltpu.make_async_remote_copy(
        src_ref=framed.at[pl.ds(64, HALO)], dst_ref=down_ref,
        send_sem=edge_send.at[1], recv_sem=edge_recv.at[1],
        device_id=(y, f - 1), device_id_type=MESH,
    )
    pl.semaphore_wait(barrier, DEVICES - 1)

    @pl.when(f < FP - 1)
    def _():
        to_next.start()

    @pl.when(f > 0)
    def _():
        to_last.start()

    for step in range(1, DEVICES):
        ty, tf = others[step - 1]
        pltpu.make_async_remote_copy(
            src_ref=meta_ref.at[ty * FP + tf], dst_ref=gmeta.at[step],
            send_sem=msend, recv_sem=mrecv,
            device_id=(ty, tf), device_id_type=MESH,
        ).start()
    top_band = band(vtap, HALO, SEG, 12)
    bottom_band = band(vtap, HALO, SEG, 44)

    @pl.when(f < FP - 1)
    def _():
        to_next.wait_send()
        to_last.wait_recv()
        framed[64 + rows : 96 + rows, :] = down_ref[...]

    @pl.when(f > 0)
    def _():
        to_last.wait_send()
        to_next.wait_recv()
        framed[32:64, :] = up_ref[...]

    made = jnp.dot(top_band, framed[32 : 32 + SEG, :], preferred_element_type=jnp.float32)
    vertical[:HALO, SEG : SEG + cols] = made.astype(jnp.bfloat16)
    made = jnp.dot(
        bottom_band, framed[rows - HALO : rows - HALO + SEG, :], preferred_element_type=jnp.float32
    )
    vertical[rows - HALO :, SEG : SEG + cols] = made.astype(jnp.bfloat16)
    edge_weight = jnp.concatenate([weight[:HALO], weight[rows - HALO :]], axis=0)
    for n in range(cols // 256):
        span = slice(n * 256, n * 256 + 512)
        both = jnp.concatenate([vertical[:HALO, span], vertical[rows - HALO :, span]], axis=0)
        made = lax.dot_general(both, hband, NT, preferred_element_type=jnp.float32)
        made = made.astype(jnp.bfloat16).astype(jnp.float32) * edge_weight
        for s in range(2):
            first = (2 * n + s) * rows
            lanes = slice(s * SEG, (s + 1) * SEG)
            pieces[first : first + HALO, :] = made[:HALO, lanes]
            pieces[first + rows - HALO : first + rows, :] = made[HALO:, lanes]
    to_scalars.wait()

    def value_copy(j, i, at):
        step = j * GROUP + i
        ty, tf = target(at, i)
        return pltpu.make_async_remote_copy(
            src_ref=sent.at[step], dst_ref=got.at[step],
            send_sem=vsend, recv_sem=vrecv.at[j],
            device_id=(ty, tf), device_id_type=MESH,
        )

    last_piece = pieces.shape[0] - 1

    def pack(j, carry):
        at = corner(j)
        for i in range(GROUP):
            ty, tf = target(at, i)
            to = ty * FP + tf
            for k in range(CAP):
                piece = jnp.clip(src_ref[to, k], 0, last_piece)
                stage[i, k : k + 1, :] = pieces[pl.ds(piece, 1), :]
            sent[j * GROUP + i] = stage[i].astype(jnp.bfloat16)
            if i:
                value_copy(j, i, at).start()
            else:

                @pl.when(j > 0)
                def _():
                    value_copy(j, 0, at).start()

                @pl.when(j == 0)
                def _():
                    own.start()

        return carry

    lax.fori_loop(0, AHEAD, pack, 0)
    span_iota = lax.broadcasted_iota(jnp.int32, (SPAN, GROUP * CAP), 0).astype(jnp.int16)
    part_iota = lax.broadcasted_iota(jnp.int32, (2 * PARTS, GROUP * CAP), 0)
    total[...] = jnp.zeros_like(total)
    weights[...] = jnp.zeros_like(weights)

    own_meta.wait()
    others_meta = gmeta.at[pl.ds(1, DEVICES - 1)]
    pltpu.make_async_copy(others_meta, others_meta, mrecv).wait()

    def arrived(j, first, count):
        slots = got.at[pl.ds(j * GROUP + first, count)]
        pltpu.make_async_copy(slots, slots, vrecv.at[j]).wait()

    def chunk(j, carry):
        @pl.when(j > 0)
        def _():
            arrived(j, 0, GROUP)

        @pl.when(j == 0)
        def _():
            own.wait()
            arrived(0, 1, GROUP - 1)

        meta = gmeta[pl.ds(j * GROUP, GROUP), 0, :]
        slots = jnp.concatenate([meta[i : i + 1, :CAP] for i in range(GROUP)], axis=1)
        weight = jnp.concatenate([meta[i : i + 1, CAP:] for i in range(GROUP)], axis=1)
        slots = slots.astype(jnp.int32)
        inside = jnp.broadcast_to(slots & (SPAN - 1), (16, GROUP * CAP)).astype(jnp.int16)
        inside = jnp.broadcast_to(inside[:1], (SPAN, GROUP * CAP))
        hot = jnp.where(span_iota == inside, jnp.bfloat16(1), jnp.bfloat16(0))
        high = weight.astype(jnp.bfloat16).astype(jnp.float32)
        part = slots >> 9
        spread = jnp.where(part_iota == part, high, 0.0)
        spread = jnp.where((part_iota == part + PARTS) & (part >= 0), weight - high, spread)
        weights[...] += lax.dot_general(
            spread.astype(jnp.bfloat16), hot, NT, preferred_element_type=jnp.float32
        )
        turned = jnp.floor(meta * (1.0 / SPAN)).T
        column = jnp.concatenate([turned[:CAP, i : i + 1] for i in range(GROUP)], axis=0)
        part = jnp.broadcast_to(column, (GROUP * CAP, SEG)).astype(jnp.bfloat16)
        values = got[pl.ds(j * GROUP, GROUP)].reshape(GROUP * CAP, SEG)
        none = jnp.zeros_like(values)
        masked = [jnp.where(part == jnp.bfloat16(a), values, none) for a in range(PARTS)]
        right = jnp.concatenate(masked, axis=1)
        total[...] += jnp.dot(hot, right, preferred_element_type=jnp.float32)
        return carry

    def both(j, carry):
        pack(j + AHEAD, carry)
        return chunk(j, carry)

    lax.fori_loop(0, groups - AHEAD, both, 0)
    lax.fori_loop(groups - AHEAD, groups, chunk, 0)

    sums = weights[:PARTS, :] + weights[PARTS:, :]
    scale = (1.0 / jnp.maximum(sums, 1.0)).T
    stores = []
    for a in range(PARTS):
        lanes = slice(a * SEG, (a + 1) * SEG)
        total[:, lanes] = total[:, lanes] * scale[:, a : a + 1]
        stores.append(
            pltpu.make_async_copy(
                total.at[:, pl.ds(a * SEG, SEG)], image_ref.at[pl.ds(a * SPAN, SPAN)], store.at[a]
            )
        )
        stores[-1].start()
        weight_ref[:, a * SPAN : (a + 1) * SPAN] = sums[a : a + 1, :]
    for copy in stores:
        copy.wait()
    for buffer, sem in ((meta_ref, msend), (sent, vsend)):
        slots = buffer.at[pl.ds(1, DEVICES - 1)]
        pltpu.make_async_copy(slots, slots, sem).wait()


def body(raw_pixels, kernel_bank, kernel_ids, inv_var, gap_start, warp_tile, warp_offset):
    raw = raw_pixels[0]
    rows, cols = raw.shape
    tiles = jnp.transpose(warp_tile[0], (1, 2, 0))
    offsets = warp_offset[0].T
    smem = pl.BlockSpec(memory_space=pltpu.SMEM)
    vmem = pl.BlockSpec(memory_space=pltpu.VMEM)
    fixed = pl.BlockSpec(memory_space=pltpu.HBM)
    dma = pltpu.SemaphoreType.DMA
    image, weight = pl.pallas_call(
        fused_kernel,
        out_shape=(
            jax.ShapeDtypeStruct((PARTS * SPAN, SEG), jnp.float32),
            jax.ShapeDtypeStruct((1, PARTS * SPAN), jnp.float32),
        ),
        in_specs=[smem, smem, smem, fixed, fixed, fixed, fixed],
        out_specs=(fixed, vmem),
        scratch_shapes=[
            pltpu.VMEM((SPAN, PARTS * SEG), jnp.float32),
            pltpu.VMEM((2 * PARTS, SPAN), jnp.float32),
            pltpu.VMEM(kernel_bank.shape, kernel_bank.dtype),
            pltpu.VMEM(tiles.shape, tiles.dtype),
            pltpu.VMEM(offsets.shape, offsets.dtype),
            pltpu.VMEM((8, 512), jnp.float32),
            pltpu.VMEM((DEVICES, 2 * CAP), jnp.int32),
            pltpu.SMEM((DEVICES, 2 * CAP), jnp.int32),
            pltpu.VMEM((DEVICES, 1, 2 * CAP), jnp.float32),
            pltpu.VMEM((HALO, cols), jnp.bfloat16),
            pltpu.VMEM((HALO, cols), jnp.bfloat16),
            pltpu.VMEM((rows + 128, cols), jnp.bfloat16),
            pltpu.VMEM((rows, cols + 2 * SEG), jnp.bfloat16),
            pltpu.VMEM((rows * cols // SEG, SEG), jnp.float32),
            pltpu.VMEM((GROUP, CAP, SEG), jnp.float32),
            pltpu.VMEM((DEVICES, CAP, SEG), jnp.bfloat16),
            pltpu.VMEM((DEVICES, CAP, SEG), jnp.bfloat16),
            pltpu.VMEM((DEVICES, 1, 2 * CAP), jnp.float32),
            dma, dma((DEVICES // GROUP,)), dma, dma, dma((2,)), dma((2,)), dma((7,)), dma((PARTS,)),
        ],
        compiler_params=pltpu.CompilerParams(
            collective_id=0, has_side_effects=True, vmem_limit_bytes=60 << 20
        ),
        name="fused",
    )(kernel_ids, inv_var, gap_start, kernel_bank, tiles, offsets, raw)
    return image[None], weight


def solution(mesh):
    in_specs = (
        P("expo", "fp", None),
        P(),
        P("expo", "fp"),
        P("expo", "fp"),
        P("expo", "fp"),
        P("expo", "fp", None, None),
        P("expo", "fp", None),
    )
    out_specs = (P(("expo", "fp"), None, None), P(("expo", "fp"), None))
    return jax.shard_map(body, mesh=mesh, in_specs=in_specs, out_specs=out_specs, check_vma=False)
```

```python
import jax
import jax.numpy as jnp
from jax import lax
from jax.experimental import pallas as pl
from jax.experimental.pallas import tpu as pltpu
from jax.sharding import PartitionSpec as P

GAP = 32
SEG = 128
CAP = 64
HALO = 32
FP = 32
DEVICES = 128
MESH = pl.DeviceIdType.MESH
NT = (((1,), (1,)), ((), ()))


def corner(group):
    y = lax.axis_index("expo")
    f = lax.axis_index("fp")
    b, c = lax.rem(group, 4), group // 4
    return y + c, f // 8 + b, lax.rem(f // 2, 4) + b + c, lax.rem(f, 2)


def target(at, i):
    y, x, z, core = at
    a = i // 2
    ty = lax.rem(y + a, 4)
    tf = lax.rem(x + a, 4) * 8 + lax.rem(z + a, 4) * 2 + lax.rem(core + i, 2)
    return ty, tf


def route(inv_ref, gap_ref, tile_ref, off_ref, src_ref, meta_ref):
    segs, _, rows = tile_ref.shape
    inv = inv_ref[0, 0]
    gap = gap_ref[0, 0]
    before = lax.broadcasted_iota(jnp.int32, (rows, rows), 0)
    after = lax.broadcasted_iota(jnp.int32, (rows, rows), 1)
    upper = (before < after).astype(jnp.float32).astype(jnp.bfloat16)
    tile_iota = lax.broadcasted_iota(jnp.int32, (DEVICES, rows), 0)
    slot_iota = lax.broadcasted_iota(jnp.int32, (CAP, rows), 0)
    row = lax.broadcasted_iota(jnp.int32, (1, rows), 1)
    open_row = jnp.where((row >= gap) & (row < gap + GAP), 0.0, 1.0)
    row_f = row.astype(jnp.float32)
    base = jnp.zeros((DEVICES, 1), jnp.float32)
    found = jnp.zeros((DEVICES, 5 * CAP), jnp.float32)
    for s in range(segs):
        hot = (tile_iota == tile_ref[s]).astype(jnp.float32)
        hot_b = hot.astype(jnp.bfloat16)
        inside = jnp.dot(hot_b, upper, preferred_element_type=jnp.float32)
        rank = jnp.sum(hot * (inside + base), axis=0, keepdims=True)
        base = base + jnp.sum(hot, axis=1, keepdims=True)
        at_slot = (slot_iota == rank.astype(jnp.int32)).astype(jnp.float32)
        offset = off_ref[s : s + 1, :] + 1
        packed = jnp.concatenate(
            [
                at_slot * float(s),
                at_slot * row_f,
                at_slot * (offset >> 6).astype(jnp.float32),
                at_slot * (offset & 63).astype(jnp.float32),
                at_slot * open_row,
            ],
            axis=0,
        ).astype(jnp.bfloat16)
        found = found + lax.dot_general(hot_b, packed, NT, preferred_element_type=jnp.float32)
    source = found[:, :CAP] * float(rows) + found[:, CAP : 2 * CAP]
    source = jnp.concatenate([source, jnp.zeros_like(source)], axis=1).astype(jnp.int32)
    src_ref[...] = jnp.clip(source, 0, segs * rows - 1)
    offset = found[:, 2 * CAP : 3 * CAP] * 64.0 + found[:, 3 * CAP : 4 * CAP] - 1.0
    meta_ref[:, 0, :] = jnp.concatenate([offset, found[:, 4 * CAP :] * inv], axis=1)


def band(taps, rows, width, shift):
    wide = jnp.broadcast_to(taps[:, :width], (rows, width))
    return pltpu.roll(wide, shift - 4, 1, stride=1, stride_axis=0).astype(jnp.bfloat16)


PARTS = 8
SPAN = 512
GROUP = 8
AHEAD = 5


def fused_kernel(
    id_ref, inv_ref, gap_ref, bank_hbm, tile_hbm, off_hbm, raw_ref, image_ref, weight_ref,
    total, weights,
    bank_ref, tile_ref, off_ref, taps_ref, slot_ref, src_ref, meta_ref, up_ref, down_ref,
    framed, vertical, pieces, stage, sent, got, gmeta,
    vsend, vrecv, msend, mrecv, edge_send, edge_recv, local, store,
):
    barrier = pltpu.get_barrier_semaphore()
    groups = DEVICES // GROUP

    y = lax.axis_index("expo")
    f = lax.axis_index("fp")
    rows, cols = raw_ref.shape
    half = SEG
    loads = [
        pltpu.make_async_copy(source, ref, local.at[n])
        for n, (source, ref) in enumerate(
            [
                (tile_hbm, tile_ref),
                (off_hbm, off_ref),
                (bank_hbm, bank_ref),
                (raw_ref, framed.at[pl.ds(64, rows)]),
            ]
        )
    ]
    for load in loads:
        load.start()
    ys = [lax.rem(y + k, 4) for k in range(4)]
    xs = [lax.rem(f // 8 + k, 4) * 8 for k in range(4)]
    zs = [lax.rem(f // 2 + k, 4) * 2 for k in range(4)]
    cores = [lax.rem(f + k, 2) for k in range(2)]
    others = []
    for step in range(1, DEVICES):
        a, b, c = step // 2 % 4, step // 8 % 4, step // 32
        to = (ys[(a + c) % 4], xs[(a + b) % 4] + zs[(a + b + c) % 4] + cores[step % 2])
        others.append(to)
        pl.semaphore_signal(barrier, inc=1, device_id=to, device_id_type=MESH)
    framed[0:64, :] = jnp.zeros((64, cols), jnp.bfloat16)
    framed[64 + rows : 128 + rows, :] = jnp.zeros((64, cols), jnp.bfloat16)
    for load in loads[:3]:
        load.wait()
    route(inv_ref, gap_ref, tile_ref, off_ref, slot_ref, meta_ref)
    to_scalars = pltpu.make_async_copy(slot_ref, src_ref, local.at[4])
    to_scalars.start()
    taps_ref[...] = jnp.zeros_like(taps_ref)
    taps_ref[0:2, 4 : 4 + bank_ref.shape[2]] = bank_ref[id_ref[0, 0]].astype(jnp.float32)
    vtap = taps_ref[0:1, :]
    htap = taps_ref[1:2, :]
    vertical[:, :SEG] = jnp.zeros((rows, SEG), jnp.bfloat16)
    vertical[:, SEG + cols :] = jnp.zeros((rows, SEG), jnp.bfloat16)
    vband = band(vtap, half, 256, 44)
    hband = band(htap, 256, 512, 108)
    loads[3].wait()
    for n in range(cols // 512):
        for m in range(rows // half):
            made = jnp.dot(
                vband,
                framed[m * half : m * half + 256, n * 512 : (n + 1) * 512],
                preferred_element_type=jnp.float32,
            )
            vertical[m * half : (m + 1) * half, SEG + n * 512 : SEG + (n + 1) * 512] = made.astype(
                jnp.bfloat16
            )
    row = lax.broadcasted_iota(jnp.int32, (rows, 256), 0)
    gap = gap_ref[0, 0]
    weight = jnp.where((row >= gap) & (row < gap + GAP), 0.0, inv_ref[0, 0])
    for n in range(cols // 256):
        made = lax.dot_general(
            vertical[:, n * 256 : n * 256 + 512], hband, NT, preferred_element_type=jnp.float32
        )
        made = made.astype(jnp.bfloat16).astype(jnp.float32) * weight
        pieces[2 * n * rows : (2 * n + 1) * rows, :] = made[:, :SEG]
        pieces[(2 * n + 1) * rows : (2 * n + 2) * rows, :] = made[:, SEG:]

    me = y * FP + f
    own_meta = pltpu.make_async_copy(meta_ref.at[me], gmeta.at[0], local.at[5])
    own = pltpu.make_async_copy(sent.at[0], got.at[0], local.at[6])
    own_meta.start()
    to_next = pltpu.make_async_remote_copy(
        src_ref=framed.at[pl.ds(32 + rows, HALO)], dst_ref=up_ref,
        send_sem=edge_send.at[0], recv_sem=edge_recv.at[0],
        device_id=(y, f + 1), device_id_type=MESH,
    )
    to_last = pltpu.make_async_remote_copy(
        src_ref=framed.at[pl.ds(64, HALO)], dst_ref=down_ref,
        send_sem=edge_send.at[1], recv_sem=edge_recv.at[1],
        device_id=(y, f - 1), device_id_type=MESH,
    )
    pl.semaphore_wait(barrier, DEVICES - 1)

    @pl.when(f < FP - 1)
    def _():
        to_next.start()

    @pl.when(f > 0)
    def _():
        to_last.start()

    for step in range(1, DEVICES):
        ty, tf = others[step - 1]
        pltpu.make_async_remote_copy(
            src_ref=meta_ref.at[ty * FP + tf], dst_ref=gmeta.at[step],
            send_sem=msend, recv_sem=mrecv,
            device_id=(ty, tf), device_id_type=MESH,
        ).start()
    top_band = band(vtap, HALO, SEG, 12)
    bottom_band = band(vtap, HALO, SEG, 44)

    @pl.when(f < FP - 1)
    def _():
        to_next.wait_send()
        to_last.wait_recv()
        framed[64 + rows : 96 + rows, :] = down_ref[...]

    @pl.when(f > 0)
    def _():
        to_last.wait_send()
        to_next.wait_recv()
        framed[32:64, :] = up_ref[...]

    made = jnp.dot(top_band, framed[32 : 32 + SEG, :], preferred_element_type=jnp.float32)
    vertical[:HALO, SEG : SEG + cols] = made.astype(jnp.bfloat16)
    made = jnp.dot(
        bottom_band, framed[rows - HALO : rows - HALO + SEG, :], preferred_element_type=jnp.float32
    )
    vertical[rows - HALO :, SEG : SEG + cols] = made.astype(jnp.bfloat16)
    edge_weight = jnp.concatenate([weight[:HALO], weight[rows - HALO :]], axis=0)
    for n in range(cols // 256):
        span = slice(n * 256, n * 256 + 512)
        both = jnp.concatenate([vertical[:HALO, span], vertical[rows - HALO :, span]], axis=0)
        made = lax.dot_general(both, hband, NT, preferred_element_type=jnp.float32)
        made = made.astype(jnp.bfloat16).astype(jnp.float32) * edge_weight
        for s in range(2):
            first = (2 * n + s) * rows
            lanes = slice(s * SEG, (s + 1) * SEG)
            pieces[first : first + HALO, :] = made[:HALO, lanes]
            pieces[first + rows - HALO : first + rows, :] = made[HALO:, lanes]
    to_scalars.wait()

    def value_copy(j, i, at):
        step = j * GROUP + i
        ty, tf = target(at, i)
        return pltpu.make_async_remote_copy(
            src_ref=sent.at[step], dst_ref=got.at[step],
            send_sem=vsend, recv_sem=vrecv.at[j],
            device_id=(ty, tf), device_id_type=MESH,
        )

    def pack(j, carry):
        at = corner(j)
        for i in range(GROUP):
            ty, tf = target(at, i)
            to = ty * FP + tf
            for k in range(CAP):
                stage[i, k : k + 1, :] = pieces[pl.ds(src_ref[to, k], 1), :]
            sent[j * GROUP + i] = stage[i].astype(jnp.bfloat16)
            if i:
                value_copy(j, i, at).start()
            else:

                @pl.when(j > 0)
                def _():
                    value_copy(j, 0, at).start()

                @pl.when(j == 0)
                def _():
                    own.start()

        return carry

    lax.fori_loop(0, AHEAD, pack, 0)
    span_iota = lax.broadcasted_iota(jnp.int32, (SPAN, GROUP * CAP), 0).astype(jnp.int16)
    part_iota = lax.broadcasted_iota(jnp.int32, (2 * PARTS, GROUP * CAP), 0)
    total[...] = jnp.zeros_like(total)
    weights[...] = jnp.zeros_like(weights)

    own_meta.wait()
    others_meta = gmeta.at[pl.ds(1, DEVICES - 1)]
    pltpu.make_async_copy(others_meta, others_meta, mrecv).wait()

    def arrived(j, first, count):
        slots = got.at[pl.ds(j * GROUP + first, count)]
        pltpu.make_async_copy(slots, slots, vrecv.at[j]).wait()

    def chunk(j, carry):
        @pl.when(j > 0)
        def _():
            arrived(j, 0, GROUP)

        @pl.when(j == 0)
        def _():
            own.wait()
            arrived(0, 1, GROUP - 1)

        meta = gmeta[pl.ds(j * GROUP, GROUP), 0, :]
        slots = jnp.concatenate([meta[i : i + 1, :CAP] for i in range(GROUP)], axis=1)
        weight = jnp.concatenate([meta[i : i + 1, CAP:] for i in range(GROUP)], axis=1)
        slots = slots.astype(jnp.int32)
        inside = jnp.broadcast_to(slots & (SPAN - 1), (16, GROUP * CAP)).astype(jnp.int16)
        inside = jnp.broadcast_to(inside[:1], (SPAN, GROUP * CAP))
        hot = jnp.where(span_iota == inside, jnp.bfloat16(1), jnp.bfloat16(0))
        high = weight.astype(jnp.bfloat16).astype(jnp.float32)
        part = slots >> 9
        spread = jnp.where(part_iota == part, high, 0.0)
        spread = jnp.where((part_iota == part + PARTS) & (part >= 0), weight - high, spread)
        weights[...] += lax.dot_general(
            spread.astype(jnp.bfloat16), hot, NT, preferred_element_type=jnp.float32
        )
        turned = jnp.floor(meta * (1.0 / SPAN)).T
        column = jnp.concatenate([turned[:CAP, i : i + 1] for i in range(GROUP)], axis=0)
        part = jnp.broadcast_to(column, (GROUP * CAP, SEG)).astype(jnp.bfloat16)
        values = got[pl.ds(j * GROUP, GROUP)].reshape(GROUP * CAP, SEG)
        none = jnp.zeros_like(values)
        masked = [jnp.where(part == jnp.bfloat16(a), values, none) for a in range(PARTS)]
        right = jnp.concatenate(masked, axis=1)
        total[...] += jnp.dot(hot, right, preferred_element_type=jnp.float32)
        return carry

    def both(j, carry):
        pack(j + AHEAD, carry)
        return chunk(j, carry)

    lax.fori_loop(0, groups - AHEAD, both, 0)
    lax.fori_loop(groups - AHEAD, groups, chunk, 0)

    sums = weights[:PARTS, :] + weights[PARTS:, :]
    scale = (1.0 / jnp.maximum(sums, 1.0)).T
    stores = []
    for a in range(PARTS):
        lanes = slice(a * SEG, (a + 1) * SEG)
        total[:, lanes] = total[:, lanes] * scale[:, a : a + 1]
        stores.append(
            pltpu.make_async_copy(
                total.at[:, pl.ds(a * SEG, SEG)], image_ref.at[pl.ds(a * SPAN, SPAN)], store.at[a]
            )
        )
        stores[-1].start()
        weight_ref[:, a * SPAN : (a + 1) * SPAN] = sums[a : a + 1, :]
    for copy in stores:
        copy.wait()
    for buffer, sem in ((meta_ref, msend), (sent, vsend)):
        slots = buffer.at[pl.ds(1, DEVICES - 1)]
        pltpu.make_async_copy(slots, slots, sem).wait()


def body(raw_pixels, kernel_bank, kernel_ids, inv_var, gap_start, warp_tile, warp_offset):
    raw = raw_pixels[0]
    rows, cols = raw.shape
    tiles = jnp.transpose(warp_tile[0], (1, 2, 0))
    offsets = warp_offset[0].T
    smem = pl.BlockSpec(memory_space=pltpu.SMEM)
    vmem = pl.BlockSpec(memory_space=pltpu.VMEM)
    fixed = pl.BlockSpec(memory_space=pltpu.HBM)
    dma = pltpu.SemaphoreType.DMA
    image, weight = pl.pallas_call(
        fused_kernel,
        out_shape=(
            jax.ShapeDtypeStruct((PARTS * SPAN, SEG), jnp.float32),
            jax.ShapeDtypeStruct((1, PARTS * SPAN), jnp.float32),
        ),
        in_specs=[smem, smem, smem, fixed, fixed, fixed, fixed],
        out_specs=(fixed, vmem),
        scratch_shapes=[
            pltpu.VMEM((SPAN, PARTS * SEG), jnp.float32),
            pltpu.VMEM((2 * PARTS, SPAN), jnp.float32),
            pltpu.VMEM(kernel_bank.shape, kernel_bank.dtype),
            pltpu.VMEM(tiles.shape, tiles.dtype),
            pltpu.VMEM(offsets.shape, offsets.dtype),
            pltpu.VMEM((8, 512), jnp.float32),
            pltpu.VMEM((DEVICES, 2 * CAP), jnp.int32),
            pltpu.SMEM((DEVICES, 2 * CAP), jnp.int32),
            pltpu.VMEM((DEVICES, 1, 2 * CAP), jnp.float32),
            pltpu.VMEM((HALO, cols), jnp.bfloat16),
            pltpu.VMEM((HALO, cols), jnp.bfloat16),
            pltpu.VMEM((rows + 128, cols), jnp.bfloat16),
            pltpu.VMEM((rows, cols + 2 * SEG), jnp.bfloat16),
            pltpu.VMEM((rows * cols // SEG, SEG), jnp.float32),
            pltpu.VMEM((GROUP, CAP, SEG), jnp.float32),
            pltpu.VMEM((DEVICES, CAP, SEG), jnp.bfloat16),
            pltpu.VMEM((DEVICES, CAP, SEG), jnp.bfloat16),
            pltpu.VMEM((DEVICES, 1, 2 * CAP), jnp.float32),
            dma, dma((DEVICES // GROUP,)), dma, dma, dma((2,)), dma((2,)), dma((7,)), dma((PARTS,)),
        ],
        compiler_params=pltpu.CompilerParams(
            collective_id=0, has_side_effects=True, vmem_limit_bytes=60 << 20
        ),
        name="fused",
    )(kernel_ids, inv_var, gap_start, kernel_bank, tiles, offsets, raw)
    return image[None], weight


def solution(mesh):
    in_specs = (
        P("expo", "fp", None),
        P(),
        P("expo", "fp"),
        P("expo", "fp"),
        P("expo", "fp"),
        P("expo", "fp", None, None),
        P("expo", "fp", None),
    )
    out_specs = (P(("expo", "fp"), None, None), P(("expo", "fp"), None))
    return jax.shard_map(body, mesh=mesh, in_specs=in_specs, out_specs=out_specs, check_vma=False)
```
